512 devices in a mesh: ctx: 32 (over z, core), head: 16 (over y, x).
Axes of the slice: x: 4, y: 4, z: 16, core: 2. Of those that a mesh axis runs over, the one named last changes fastest.
Arguments:
- queries: bfloat16 [8192, 8192], P('ctx', 'head'), may hold values from -6 to 6
- keys: bfloat16 [8192, 8192], P('ctx', 'head'), may hold values from -6 to 6
- values: bfloat16 [8192, 8192], P('ctx', 'head'), may hold values from -6 to 6
- out_weight: bfloat16 [8192, 6144], P('head', 'ctx'), may hold values from -0.0625 to 0.0625
Outputs:
- output: bfloat16 [8192, 6144], P('ctx', 'head')
The draws below stay inside these ranges and needn't reach their ends.
All inputs are finite; a program needn't handle non-finite values.
Results may differ from the reference program's by a relative error of at most 0.022.
Values may be sent and summed in bfloat16 or wider, within the bound.
No kernel may reach another device: no remote copies, remote signals or barrier semaphores. Data moves between devices by JAX's collectives and lax.ppermute only.
A program may use at most 64 MiB of HBM per device.

```python
import jax
import jax.numpy as jnp
from jax import lax

D = 6144
HEADS = 64
DH = 128
TOK_DEV = 256
TOKENS = 8192
WIDTH = 8192
N_CTX = 32
N_HEAD = 16


def shard_levels(key, dims, split, low, high):
    factor_of, own = 1.0, jax.random.fold_in(key, 6)
    for dim, parts in split:
        draws = jnp.exp(jax.random.uniform(jax.random.fold_in(own, dim), (parts,), jnp.float32, low / len(split), high / len(split)))
        factor_of = factor_of * jnp.repeat(draws, dims[dim] // parts).reshape([-1 if axis == dim else 1 for axis in range(len(dims))])
    return factor_of


def gaussian(stream_key, dims, spread, reach, cuts=(), held_as=jnp.bfloat16):
    drawn = spread * jax.random.normal(stream_key, dims, jnp.float32)
    if cuts:
        drawn = drawn * shard_levels(stream_key, dims, cuts, -0.22, 0.18)
    return jnp.clip(drawn, -reach, reach).astype(held_as)


def setup_inputs(seed: int = 0) -> dict:
    seeds = jax.random.split(jax.random.key(seed), 5)
    return {
        "queries": gaussian(seeds[0], (TOKENS, WIDTH), 1.0, 6.0, ((0, 32), (1, 16))),
        "keys": gaussian(seeds[1], (TOKENS, WIDTH), 1.0, 6.0, ((0, 32), (1, 16))),
        "values": gaussian(seeds[2], (TOKENS, WIDTH), 1.0, 6.0, ((0, 32), (1, 16))),
        "out_weight": gaussian(seeds[3], (WIDTH, D), WIDTH ** -0.5, 0.0625, ((0, 16), (1, 32))),
    }


def reference(queries, keys, values, out_weight):
    shape = (N_CTX, TOK_DEV, HEADS, DH)
    q = queries.reshape(shape)
    k = keys.reshape(shape)
    v = values.reshape(shape)
    states = jnp.einsum('bthd,bthe->bhde', k.astype(jnp.float32), v.astype(jnp.float32)).astype(jnp.bfloat16)
    running = jnp.cumsum(states.astype(jnp.float32), axis=0)
    prefix = jnp.concatenate([jnp.zeros_like(running[:1]), running[:-1]], axis=0).astype(jnp.bfloat16)
    rows = jnp.arange(TOK_DEV)
    causal = rows[:, None] >= rows[None, :]

    def one_block(items):
        qb, kb, vb, pb, index = items
        scores = jnp.einsum('thd,shd->hts', qb.astype(jnp.float32), kb.astype(jnp.float32))
        scores = jnp.where(causal[None], scores, 0.0).astype(jnp.bfloat16)
        intra = jnp.einsum('hts,she->the', scores.astype(jnp.float32), vb.astype(jnp.float32))
        inter = jnp.einsum('thd,hde->the', qb.astype(jnp.float32), pb.astype(jnp.float32))
        position = (index * TOK_DEV + rows).astype(jnp.float32)
        scale = jnp.sqrt(DH * (position + 1.0))
        return ((intra + inter) / scale[:, None, None]).astype(jnp.bfloat16)
    attended = lax.map(one_block, (q, k, v, prefix, jnp.arange(N_CTX, dtype=jnp.int32)))
    attended = attended.reshape(TOKENS, WIDTH)
    group = WIDTH // N_HEAD
    total = jnp.zeros((TOKENS, D), jnp.float32)
    for index in range(N_HEAD):
        term = jnp.dot(attended[:, index * group:(index + 1) * group], out_weight[index * group:(index + 1) * group], preferred_element_type=jnp.float32)
        total = total + term.astype(jnp.bfloat16).astype(jnp.float32)
    return total.astype(jnp.bfloat16)
```

```python
import functools

import jax
import jax.numpy as jnp
from jax import lax
from jax.experimental import pallas as pl
from jax.experimental.pallas import tpu as pltpu
from jax.sharding import Mesh
from jax.sharding import PartitionSpec as P

DH = 128
BF16 = jnp.bfloat16
F32 = jnp.float32
GRID = {"za": 4, "zb": 2, "zc": 2, "core": 2, "y": 4, "x": 4}
AXES = tuple(GRID)
CTX = ("za", "zb", "zc", "core")
HEAD = ("y", "x")
NEAR = ("zb", "zc", "core")
VMEM = pltpu.CompilerParams(vmem_limit_bytes=32 * 1024 * 1024)


def dot(a, b, dims):
    return lax.dot_general(a, b, (dims, ((), ())), preferred_element_type=F32)


def state_kernel(k_ref, v_ref, out_ref):
    for h in range(k_ref.shape[1] // DH):
        cols = pl.ds(h * DH, DH)
        out_ref[cols, :] = dot(k_ref[:, cols], v_ref[:, cols], ((0,), (0,))).astype(BF16)


def block_states(k, v):
    return pl.pallas_call(
        state_kernel,
        out_shape=jax.ShapeDtypeStruct((k.shape[1], DH), BF16),
        compiler_params=VMEM,
        name="block_state",
    )(k, v)


def attend_kernel(index_ref, q_ref, k_ref, v_ref, prefix_ref, out_ref):
    rows = q_ref.shape[0]
    causal = lax.broadcasted_iota(jnp.int32, (rows, rows), 0) >= lax.broadcasted_iota(
        jnp.int32, (rows, rows), 1
    )
    position = index_ref[0] * rows + lax.broadcasted_iota(jnp.int32, (rows, DH), 0)
    scale = jnp.sqrt(DH * (position.astype(F32) + 1.0))
    for h in range(q_ref.shape[1] // DH):
        cols = pl.ds(h * DH, DH)
        q = q_ref[:, cols]
        scores = jnp.where(causal, dot(q, k_ref[:, cols], ((1,), (1,))), 0.0).astype(BF16)
        both = dot(scores, v_ref[:, cols], ((1,), (0,))) + dot(q, prefix_ref[cols, :], ((1,), (0,)))
        attended = (both / scale).astype(BF16)
        for copy in range(out_ref.shape[0]):
            out_ref[copy, :, cols] = attended


def attend(index, q, k, v, prefix, copies):
    whole = pl.BlockSpec(memory_space=pltpu.VMEM)
    return pl.pallas_call(
        attend_kernel,
        out_shape=jax.ShapeDtypeStruct((copies, *q.shape), BF16),
        in_specs=[pl.BlockSpec(memory_space=pltpu.SMEM)] + [whole] * 4,
        out_specs=whole,
        compiler_params=VMEM,
        name="attend",
    )(index, q, k, v, prefix)


def project_kernel(w_ref, a_ref, out_ref):
    for t in range(a_ref.shape[0]):
        total = dot(w_ref[0, 0], a_ref[t, 0], ((1,), (1,)))
        for g in range(1, a_ref.shape[1]):
            total += dot(w_ref[0, g], a_ref[t, g], ((1,), (1,)))
        out_ref[t, 0] = total.astype(BF16)


def project(weight, attended):
    chunks, groups, columns, width = weight.shape
    blocks, _, tokens, _ = attended.shape
    return pl.pallas_call(
        project_kernel,
        grid=(chunks,),
        out_shape=jax.ShapeDtypeStruct((blocks, chunks, columns, tokens), BF16),
        in_specs=[
            pl.BlockSpec((1, groups, columns, width), lambda i: (i, 0, 0, 0)),
            pl.BlockSpec((blocks, groups, tokens, width), lambda i: (0, 0, 0, 0)),
        ],
        out_specs=pl.BlockSpec((blocks, 1, columns, tokens), lambda i: (0, i, 0, 0)),
        compiler_params=VMEM,
        name="project",
    )(weight, attended)


def finish_kernel(parts_ref, out_ref):
    halves, terms, columns, tokens = parts_ref.shape
    for half in range(halves):
        total = parts_ref[half, 0].astype(F32)
        for term in range(1, terms):
            total += parts_ref[half, term].astype(F32)
        out_ref[pl.ds(half * columns, columns), :] = total.astype(BF16)


def finish(parts):
    halves, _, columns, tokens = parts.shape
    return pl.pallas_call(
        finish_kernel,
        out_shape=jax.ShapeDtypeStruct((halves * columns, tokens), BF16),
        compiler_params=VMEM,
        name="finish",
    )(parts)


def flat(**at):
    index = 0
    for axis, size in GRID.items():
        index = index * size + at[axis]
    return index


def weight_moves():
    pairs = []
    for za in range(4):
        for zj in range(4):
            for core in range(2):
                for y in range(4):
                    for x in range(4):
                        source = flat(za=za, zb=zj // 2, zc=zj % 2, core=core, y=y, x=x)
                        target = flat(za=za, zb=x // 2, zc=core, core=x % 2, y=y, x=zj)
                        pairs.append((source, target))
    return pairs


def earlier_states(state):
    rows = state.shape[0] // 8
    pieces = lax.all_to_all(state.reshape(8, rows, DH), NEAR, 0, 0)
    pieces = pieces.astype(F32)
    running = jnp.cumsum(pieces, axis=0)
    total = running[-1]
    before = running - pieces
    totals = lax.all_gather(total.astype(BF16), "za").astype(F32)
    reached = jnp.arange(GRID["za"])[:, None, None] < lax.axis_index("za")
    carried = jnp.sum(jnp.where(reached, totals, 0.0), axis=0)
    prefix = (before + carried[None]).astype(BF16)
    return lax.all_to_all(prefix, NEAR, 0, 0).reshape(state.shape)


def per_device(queries, keys, values, out_weight):
    tokens, width = queries.shape
    columns = out_weight.shape[1]
    moved = lax.ppermute(out_weight.T, AXES, weight_moves())
    weight = lax.all_gather(moved, ("za", "zb", "core"))
    weight = weight.reshape(GRID["y"], GRID["x"], columns, width)

    prefix = earlier_states(block_states(keys, values))
    index = lax.axis_index(CTX).astype(jnp.int32).reshape(1)
    attended = attend(index, queries, keys, values, prefix, GRID["zc"] * GRID["x"])
    attended = lax.all_to_all(attended, ("zc", "x"), 0, 0)
    attended = attended.reshape(GRID["zc"], GRID["x"], tokens, width)
    partial = project(weight, attended)
    partial = partial.reshape(GRID["zc"] * GRID["y"], columns, tokens)
    parts = lax.all_to_all(partial, ("zc", "y"), 0, 0)
    return finish(parts.reshape(GRID["zc"], GRID["y"], columns, tokens)).T


def solution(mesh):
    grid = Mesh(mesh.devices.reshape(tuple(GRID.values())), AXES)
    spec = P(CTX, HEAD)
    return jax.shard_map(
        per_device,
        mesh=grid,
        in_specs=(spec, spec, spec, P(HEAD, CTX)),
        out_specs=spec,
        check_vma=False,
    )
```

```python
import functools

import jax
import jax.numpy as jnp
from jax import lax
from jax.experimental import pallas as pl
from jax.experimental.pallas import tpu as pltpu
from jax.sharding import Mesh
from jax.sharding import PartitionSpec as P

DH = 128
BF16 = jnp.bfloat16
F32 = jnp.float32
GRID = {"za": 4, "zb": 2, "zc": 2, "core": 2, "y": 4, "x": 4}
AXES = tuple(GRID)
CTX = ("za", "zb", "zc", "core")
HEAD = ("y", "x")
NEAR = ("zb", "zc", "core")
VMEM = pltpu.CompilerParams(vmem_limit_bytes=32 * 1024 * 1024)


def dot(a, b, dims):
    return lax.dot_general(a, b, (dims, ((), ())), preferred_element_type=F32)


def state_kernel(k_ref, v_ref, out_ref):
    for h in range(k_ref.shape[1] // DH):
        cols = pl.ds(h * DH, DH)
        out_ref[cols, :] = dot(k_ref[:, cols], v_ref[:, cols], ((0,), (0,))).astype(BF16)


def block_states(k, v):
    return pl.pallas_call(
        state_kernel,
        out_shape=jax.ShapeDtypeStruct((k.shape[1], DH), BF16),
        compiler_params=VMEM,
        name="block_state",
    )(k, v)


def attend_kernel(index_ref, q_ref, k_ref, v_ref, prefix_ref, out_ref):
    rows = q_ref.shape[0]
    causal = lax.broadcasted_iota(jnp.int32, (rows, rows), 0) >= lax.broadcasted_iota(
        jnp.int32, (rows, rows), 1
    )
    position = index_ref[0] * rows + lax.broadcasted_iota(jnp.int32, (rows, DH), 0)
    scale = jnp.sqrt(DH * (position.astype(F32) + 1.0))
    for h in range(q_ref.shape[1] // DH):
        cols = pl.ds(h * DH, DH)
        q = q_ref[:, cols]
        scores = jnp.where(causal, dot(q, k_ref[:, cols], ((1,), (1,))), 0.0).astype(BF16)
        both = dot(scores, v_ref[:, cols], ((1,), (0,))) + dot(q, prefix_ref[cols, :], ((1,), (0,)))
        attended = (both / scale).astype(BF16)
        for copy in range(out_ref.shape[0]):
            out_ref[copy, :, cols] = attended


def attend(index, q, k, v, prefix, copies):
    whole = pl.BlockSpec(memory_space=pltpu.VMEM)
    return pl.pallas_call(
        attend_kernel,
        out_shape=jax.ShapeDtypeStruct((copies, *q.shape), BF16),
        in_specs=[pl.BlockSpec(memory_space=pltpu.SMEM)] + [whole] * 4,
        out_specs=whole,
        compiler_params=VMEM,
        name="attend",
    )(index, q, k, v, prefix)


def project_kernel(w_ref, a_ref, out_ref):
    for t in range(a_ref.shape[0]):
        total = dot(w_ref[0, 0], a_ref[t, 0], ((1,), (1,)))
        for g in range(1, a_ref.shape[1]):
            total += dot(w_ref[0, g], a_ref[t, g], ((1,), (1,)))
        out_ref[t, 0] = total.astype(BF16)


def project(weight, attended):
    chunks, groups, columns, width = weight.shape
    blocks, _, tokens, _ = attended.shape
    return pl.pallas_call(
        project_kernel,
        grid=(chunks,),
        out_shape=jax.ShapeDtypeStruct((blocks, chunks, columns, tokens), BF16),
        in_specs=[
            pl.BlockSpec((1, groups, columns, width), lambda i: (i, 0, 0, 0)),
            pl.BlockSpec((blocks, groups, tokens, width), lambda i: (0, 0, 0, 0)),
        ],
        out_specs=pl.BlockSpec((blocks, 1, columns, tokens), lambda i: (0, i, 0, 0)),
        compiler_params=VMEM,
        name="project",
    )(weight, attended)


def finish_kernel(parts_ref, out_ref):
    halves, terms, columns, tokens = parts_ref.shape
    for half in range(halves):
        total = parts_ref[half, 0].astype(F32)
        for term in range(1, terms):
            total += parts_ref[half, term].astype(F32)
        out_ref[pl.ds(half * columns, columns), :] = total.astype(BF16)


def finish(parts):
    halves, _, columns, tokens = parts.shape
    return pl.pallas_call(
        finish_kernel,
        out_shape=jax.ShapeDtypeStruct((halves * columns, tokens), BF16),
        compiler_params=VMEM,
        name="finish",
    )(parts)


def flat(**at):
    index = 0
    for axis, size in GRID.items():
        index = index * size + at[axis]
    return index


def weight_moves():
    pairs = []
    for za in range(4):
        for zj in range(4):
            for core in range(2):
                for y in range(4):
                    for x in range(4):
                        source = flat(za=za, zb=zj // 2, zc=zj % 2, core=core, y=y, x=x)
                        target = flat(za=za, zb=x // 2, zc=x % 2, core=core, y=y, x=zj)
                        pairs.append((source, target))
    return pairs


def earlier_states(state):
    rows = state.shape[0] // 8
    pieces = lax.all_to_all(state.reshape(8, rows, DH), NEAR, 0, 0)
    pieces = pieces.astype(F32)
    running = jnp.cumsum(pieces, axis=0)
    total = running[-1]
    before = running - pieces
    totals = lax.all_gather(total.astype(BF16), "za").astype(F32)
    reached = jnp.arange(GRID["za"])[:, None, None] < lax.axis_index("za")
    carried = jnp.sum(jnp.where(reached, totals, 0.0), axis=0)
    prefix = (before + carried[None]).astype(BF16)
    return lax.all_to_all(prefix, NEAR, 0, 0).reshape(state.shape)


def per_device(queries, keys, values, out_weight):
    tokens, width = queries.shape
    columns = out_weight.shape[1]
    moved = lax.ppermute(out_weight.T, AXES, weight_moves())
    weight = lax.all_gather(moved, CTX)
    weight = weight.reshape(GRID["y"], GRID["x"], 2 * columns, width)

    prefix = earlier_states(block_states(keys, values))
    index = lax.axis_index(CTX).astype(jnp.int32).reshape(1)
    attended = attend(index, queries, keys, values, prefix, GRID["x"])
    attended = lax.all_to_all(attended, "x", 0, 0)
    attended = attended.reshape(1, GRID["x"], tokens, width)
    partial = project(weight, attended)
    partial = partial.reshape(GRID["y"], 2 * columns, tokens)
    parts = lax.all_to_all(partial, "y", 0, 0)
    return finish(parts.reshape(1, GRID["y"], 2 * columns, tokens)).T


def solution(mesh):
    grid = Mesh(mesh.devices.reshape(tuple(GRID.values())), AXES)
    spec = P(CTX, HEAD)
    return jax.shard_map(
        per_device,
        mesh=grid,
        in_specs=(spec, spec, spec, P(HEAD, CTX)),
        out_specs=spec,
        check_vma=False,
    )
```

```python
import functools

import jax
import jax.numpy as jnp
from jax import lax
from jax.experimental import pallas as pl
from jax.experimental.pallas import tpu as pltpu
from jax.sharding import Mesh
from jax.sharding import PartitionSpec as P

DH = 128
BF16 = jnp.bfloat16
F32 = jnp.float32
GRID = {"za": 4, "zb": 2, "zc": 2, "core": 2, "y": 4, "x": 4}
AXES = tuple(GRID)
CTX = ("za", "zb", "zc", "core")
HEAD = ("y", "x")
NEAR = ("zb", "zc", "core")
VMEM = pltpu.CompilerParams(vmem_limit_bytes=32 * 1024 * 1024)


def dot(a, b, dims):
    return lax.dot_general(a, b, (dims, ((), ())), preferred_element_type=F32)


def state_kernel(k_ref, v_ref, out_ref):
    for h in range(k_ref.shape[1] // DH):
        cols = pl.ds(h * DH, DH)
        out_ref[cols, :] = dot(k_ref[:, cols], v_ref[:, cols], ((0,), (0,))).astype(BF16)


def block_states(k, v):
    return pl.pallas_call(
        state_kernel,
        out_shape=jax.ShapeDtypeStruct((k.shape[1], DH), BF16),
        compiler_params=VMEM,
        name="block_state",
    )(k, v)


def attend_kernel(index_ref, q_ref, k_ref, v_ref, prefix_ref, out_ref):
    rows = q_ref.shape[0]
    causal = lax.broadcasted_iota(jnp.int32, (rows, rows), 0) >= lax.broadcasted_iota(
        jnp.int32, (rows, rows), 1
    )
    position = index_ref[0] * rows + lax.broadcasted_iota(jnp.int32, (rows, DH), 0)
    scale = jnp.sqrt(DH * (position.astype(F32) + 1.0))
    for h in range(q_ref.shape[1] // DH):
        cols = pl.ds(h * DH, DH)
        q = q_ref[:, cols]
        scores = jnp.where(causal, dot(q, k_ref[:, cols], ((1,), (1,))), 0.0).astype(BF16)
        both = dot(scores, v_ref[:, cols], ((1,), (0,))) + dot(q, prefix_ref[cols, :], ((1,), (0,)))
        attended = (both / scale).T.astype(BF16)
        for copy in range(out_ref.shape[0]):
            out_ref[copy, cols, :] = attended


def attend(index, q, k, v, prefix, copies):
    whole = pl.BlockSpec(memory_space=pltpu.VMEM)
    return pl.pallas_call(
        attend_kernel,
        out_shape=jax.ShapeDtypeStruct((copies, q.shape[1], q.shape[0]), BF16),
        in_specs=[pl.BlockSpec(memory_space=pltpu.SMEM)] + [whole] * 4,
        out_specs=whole,
        compiler_params=VMEM,
        name="attend",
    )(index, q, k, v, prefix)


def project_kernel(w_ref, a_ref, out_ref):
    shards, groups, columns, width = w_ref.shape
    together = 8
    rows = together * columns
    for i in range(0, shards, together):
        total = dot(w_ref[i : i + together, 0].reshape(rows, width), a_ref[0], ((1,), (0,)))
        for g in range(1, groups):
            part = w_ref[i : i + together, g].reshape(rows, width)
            total += dot(part, a_ref[g], ((1,), (0,)))
        out_ref[pl.ds(i * columns, rows), :] = total.astype(BF16)


def project(weight, attended):
    shards, groups, columns, width = weight.shape
    return pl.pallas_call(
        project_kernel,
        out_shape=jax.ShapeDtypeStruct((shards * columns, attended.shape[2]), BF16),
        compiler_params=VMEM,
        name="project",
    )(weight, attended)


def finish_kernel(parts_ref, out_ref):
    for half in range(parts_ref.shape[2]):
        for x in range(parts_ref.shape[1]):
            total = parts_ref[0, x, half].astype(F32)
            for y in range(1, parts_ref.shape[0]):
                total += parts_ref[y, x, half].astype(F32)
            columns = total.shape[0]
            place = (half * parts_ref.shape[1] + x) * columns
            out_ref[pl.ds(place, columns), :] = total


def turn_kernel(parts_ref, out_ref, total_ref):
    finish_kernel(parts_ref, total_ref)
    out_ref[...] = total_ref[...].T.astype(BF16)


def finish(parts):
    _, x, halves, columns, tokens = parts.shape
    total = x * halves * columns
    return pl.pallas_call(
        turn_kernel,
        out_shape=jax.ShapeDtypeStruct((tokens, total), BF16),
        scratch_shapes=[pltpu.VMEM((total, tokens), F32)],
        compiler_params=VMEM,
        name="finish",
    )(parts)


def earlier_states(state):
    rows = state.shape[0] // 8
    pieces = lax.all_to_all(state.reshape(8, rows, DH), NEAR, 0, 0)
    pieces = pieces.astype(F32)
    running = jnp.cumsum(pieces, axis=0)
    total = running[-1]
    before = running - pieces
    totals = lax.all_gather(total.astype(BF16), "za").astype(F32)
    reached = jnp.arange(GRID["za"])[:, None, None] < lax.axis_index("za")
    carried = jnp.sum(jnp.where(reached, totals, 0.0), axis=0)
    prefix = (before + carried[None]).astype(BF16)
    return lax.all_to_all(prefix, NEAR, 0, 0).reshape(state.shape)


def per_device(queries, keys, values, out_weight):
    tokens, width = queries.shape
    groups = GRID["x"]
    columns = out_weight.shape[1] // groups
    weight = lax.all_to_all(out_weight.T.reshape(groups, columns, width), "x", 0, 0)
    weight = lax.all_gather(weight, CTX)

    states = block_states(keys, values)
    index = lax.axis_index(CTX).astype(jnp.int32).reshape(1)

    def gathered(states):
        prefix = earlier_states(states)
        attended = attend(index, queries, keys, values, prefix, groups)
        return lax.all_to_all(attended, "x", 0, 0)

    def nothing(states):
        return jnp.zeros((groups, width, tokens), BF16)

    attended = lax.cond(lax.axis_index(CTX) < 64, gathered, nothing, states)
    partial = project(weight, attended)
    owners = GRID["y"] * GRID["x"]
    parts = lax.all_to_all(partial.reshape(owners, 2 * columns, tokens), HEAD, 0, 0)
    return finish(parts.reshape(GRID["y"], GRID["x"], 2, columns, tokens))


def solution(mesh):
    grid = Mesh(mesh.devices.reshape(tuple(GRID.values())), AXES)
    spec = P(CTX, HEAD)
    return jax.shard_map(
        per_device,
        mesh=grid,
        in_specs=(spec, spec, spec, P(HEAD, CTX)),
        out_specs=spec,
        check_vma=False,
    )
```

```python
import functools

import jax
import jax.numpy as jnp
from jax import lax
from jax.experimental import pallas as pl
from jax.experimental.pallas import tpu as pltpu
from jax.sharding import Mesh
from jax.sharding import PartitionSpec as P

DH = 128
BF16 = jnp.bfloat16
F32 = jnp.float32
GRID = {"za": 4, "zb": 2, "zc": 2, "core": 2, "y": 4, "x": 4}
AXES = tuple(GRID)
CTX = ("za", "zb", "zc", "core")
HEAD = ("y", "x")
NEAR = ("zb", "zc", "core")
VMEM = pltpu.CompilerParams(vmem_limit_bytes=32 * 1024 * 1024)


def dot(a, b, dims):
    return lax.dot_general(a, b, (dims, ((), ())), preferred_element_type=F32)


def state_kernel(k_ref, v_ref, out_ref):
    for h in range(k_ref.shape[1] // DH):
        cols = pl.ds(h * DH, DH)
        out_ref[cols, :] = dot(k_ref[:, cols], v_ref[:, cols], ((0,), (0,))).astype(BF16)


def block_states(k, v):
    return pl.pallas_call(
        state_kernel,
        out_shape=jax.ShapeDtypeStruct((k.shape[1], DH), BF16),
        compiler_params=VMEM,
        name="block_state",
    )(k, v)


def attend_kernel(index_ref, q_ref, k_ref, v_ref, prefix_ref, out_ref):
    rows = q_ref.shape[0]
    causal = lax.broadcasted_iota(jnp.int32, (rows, rows), 0) >= lax.broadcasted_iota(
        jnp.int32, (rows, rows), 1
    )
    position = index_ref[0] * rows + lax.broadcasted_iota(jnp.int32, (rows, DH), 0)
    scale = jnp.sqrt(DH * (position.astype(F32) + 1.0))
    for h in range(q_ref.shape[1] // DH):
        cols = pl.ds(h * DH, DH)
        q = q_ref[:, cols]
        scores = jnp.where(causal, dot(q, k_ref[:, cols], ((1,), (1,))), 0.0).astype(BF16)
        both = dot(scores, v_ref[:, cols], ((1,), (0,))) + dot(q, prefix_ref[cols, :], ((1,), (0,)))
        attended = (both / scale).T.astype(BF16)
        for copy in range(out_ref.shape[0]):
            out_ref[copy, cols, :] = attended


def attend(index, q, k, v, prefix, copies):
    whole = pl.BlockSpec(memory_space=pltpu.VMEM)
    return pl.pallas_call(
        attend_kernel,
        out_shape=jax.ShapeDtypeStruct((copies, q.shape[1], q.shape[0]), BF16),
        in_specs=[pl.BlockSpec(memory_space=pltpu.SMEM)] + [whole] * 4,
        out_specs=whole,
        compiler_params=VMEM,
        name="attend",
    )(index, q, k, v, prefix)


def project_kernel(core_ref, w_ref, own_ref, other_ref, out_ref):
    shards, groups, columns, width = w_ref.shape
    together = 8
    rows = together * columns
    for which, a_ref in enumerate((own_ref, other_ref)):
        place = lax.bitwise_xor(core_ref[0], which)
        for i in range(0, shards, together):
            total = dot(w_ref[i : i + together, 0].reshape(rows, width), a_ref[0], ((1,), (0,)))
            for g in range(1, groups):
                part = w_ref[i : i + together, g].reshape(rows, width)
                total += dot(part, a_ref[g], ((1,), (0,)))
            out_ref[place, i : i + together] = total.astype(BF16).reshape(together, columns, -1)


def project(core, weight, own, other):
    shards, _, columns, _ = weight.shape
    vmem = pl.BlockSpec(memory_space=pltpu.VMEM)
    return pl.pallas_call(
        project_kernel,
        out_shape=jax.ShapeDtypeStruct((2, shards, columns, own.shape[2]), BF16),
        in_specs=[pl.BlockSpec(memory_space=pltpu.SMEM)] + [vmem] * 3,
        out_specs=vmem,
        compiler_params=VMEM,
        name="project",
    )(core, weight, own, other)


def finish_kernel(parts_ref, out_ref):
    for half in range(parts_ref.shape[0]):
        for x in range(parts_ref.shape[2]):
            total = parts_ref[half, 0, x].astype(F32)
            for y in range(1, parts_ref.shape[1]):
                total += parts_ref[half, y, x].astype(F32)
            columns = total.shape[0]
            place = (half * parts_ref.shape[2] + x) * columns
            out_ref[pl.ds(place, columns), :] = total


def turn_kernel(parts_ref, out_ref, total_ref):
    finish_kernel(parts_ref, total_ref)
    out_ref[...] = total_ref[...].T.astype(BF16)


def finish(parts):
    halves, _, x, columns, tokens = parts.shape
    total = x * halves * columns
    return pl.pallas_call(
        turn_kernel,
        out_shape=jax.ShapeDtypeStruct((tokens, total), BF16),
        scratch_shapes=[pltpu.VMEM((total, tokens), F32)],
        compiler_params=VMEM,
        name="finish",
    )(parts)


def earlier_states(state):
    rows = state.shape[0] // 8
    pieces = lax.all_to_all(state.reshape(8, rows, DH), NEAR, 0, 0)
    pieces = pieces.astype(F32)
    running = jnp.cumsum(pieces, axis=0)
    total = running[-1]
    before = running - pieces
    totals = lax.all_gather(total.astype(BF16), "za").astype(F32)
    reached = jnp.arange(GRID["za"])[:, None, None] < lax.axis_index("za")
    carried = jnp.sum(jnp.where(reached, totals, 0.0), axis=0)
    prefix = (before + carried[None]).astype(BF16)
    return lax.all_to_all(prefix, NEAR, 0, 0).reshape(state.shape)


def per_device(queries, keys, values, out_weight):
    tokens, width = queries.shape
    groups = GRID["x"]
    columns = out_weight.shape[1] // groups
    weight = lax.all_to_all(out_weight.T.reshape(groups, columns, width), "x", 0, 0)
    weight = lax.all_gather(weight, ("za", "zb", "zc"))

    states = block_states(keys, values)
    index = lax.axis_index(CTX).astype(jnp.int32).reshape(1)

    def gathered(states):
        prefix = earlier_states(states)
        attended = attend(index, queries, keys, values, prefix, groups)
        return lax.all_to_all(attended, "x", 0, 0)

    def nothing(states):
        return jnp.zeros((groups, width, tokens), BF16)

    attended = lax.cond(lax.axis_index(CTX) < 64, gathered, nothing, states)
    other = lax.ppermute(attended, "core", [(0, 1), (1, 0)])
    core = lax.axis_index("core").astype(jnp.int32).reshape(1)
    partial = project(core, weight, attended, other)
    parts = lax.all_to_all(partial.reshape(32, columns, tokens), ("core",) + HEAD, 0, 0)
    return finish(parts.reshape(2, GRID["y"], GRID["x"], columns, tokens))


def solution(mesh):
    grid = Mesh(mesh.devices.reshape(tuple(GRID.values())), AXES)
    spec = P(CTX, HEAD)
    return jax.shard_map(
        per_device,
        mesh=grid,
        in_specs=(spec, spec, spec, P(HEAD, CTX)),
        out_specs=spec,
        check_vma=False,
    )
```

```python
import functools

import jax
import jax.numpy as jnp
from jax import lax
from jax.experimental import pallas as pl
from jax.experimental.pallas import tpu as pltpu
from jax.sharding import Mesh
from jax.sharding import PartitionSpec as P

DH = 128
BF16 = jnp.bfloat16
F32 = jnp.float32
GRID = {"za": 4, "zb": 2, "zc": 2, "core": 2, "y": 4, "x": 4}
AXES = tuple(GRID)
CTX = ("za", "zb", "zc", "core")
HEAD = ("y", "x")
NEAR = ("zb", "zc", "core")
VMEM = pltpu.CompilerParams(vmem_limit_bytes=32 * 1024 * 1024)


def dot(a, b, dims):
    return lax.dot_general(a, b, (dims, ((), ())), preferred_element_type=F32)


def state_kernel(k_ref, v_ref, out_ref):
    for h in range(k_ref.shape[1] // DH):
        cols = pl.ds(h * DH, DH)
        out_ref[cols, :] = dot(k_ref[:, cols], v_ref[:, cols], ((0,), (0,))).astype(BF16)


def block_states(k, v):
    return pl.pallas_call(
        state_kernel,
        out_shape=jax.ShapeDtypeStruct((k.shape[1], DH), BF16),
        compiler_params=VMEM,
        name="block_state",
    )(k, v)


def attend_kernel(index_ref, q_ref, k_ref, v_ref, prefix_ref, out_ref):
    rows = q_ref.shape[0]
    causal = lax.broadcasted_iota(jnp.int32, (rows, rows), 0) >= lax.broadcasted_iota(
        jnp.int32, (rows, rows), 1
    )
    position = index_ref[0] * rows + lax.broadcasted_iota(jnp.int32, (rows, DH), 0)
    scale = jnp.sqrt(DH * (position.astype(F32) + 1.0))
    for h in range(q_ref.shape[1] // DH):
        cols = pl.ds(h * DH, DH)
        q = q_ref[:, cols]
        scores = jnp.where(causal, dot(q, k_ref[:, cols], ((1,), (1,))), 0.0).astype(BF16)
        both = dot(scores, v_ref[:, cols], ((1,), (0,))) + dot(q, prefix_ref[cols, :], ((1,), (0,)))
        attended = (both / scale).T.astype(BF16)
        for copy in range(out_ref.shape[0]):
            out_ref[copy, cols, :] = attended


def attend(index, q, k, v, prefix, copies):
    whole = pl.BlockSpec(memory_space=pltpu.VMEM)
    return pl.pallas_call(
        attend_kernel,
        out_shape=jax.ShapeDtypeStruct((copies, q.shape[1], q.shape[0]), BF16),
        in_specs=[pl.BlockSpec(memory_space=pltpu.SMEM)] + [whole] * 4,
        out_specs=whole,
        compiler_params=VMEM,
        name="attend",
    )(index, q, k, v, prefix)


def project_kernel(core_ref, w_ref, own_ref, other_ref, out_ref):
    shards, groups, columns, width = w_ref.shape
    together = 8
    rows = together * columns
    for which, a_ref in enumerate((own_ref, other_ref)):
        place = lax.bitwise_xor(core_ref[0], which)
        for i in range(0, shards, together):
            total = dot(w_ref[i : i + together, 0].reshape(rows, width), a_ref[0], ((1,), (0,)))
            for g in range(1, groups):
                part = w_ref[i : i + together, g].reshape(rows, width)
                total += dot(part, a_ref[g], ((1,), (0,)))
            out_ref[place, i : i + together] = total.astype(BF16).reshape(together, columns, -1)


def project(core, weight, own, other):
    shards, _, columns, _ = weight.shape
    vmem = pl.BlockSpec(memory_space=pltpu.VMEM)
    return pl.pallas_call(
        project_kernel,
        out_shape=jax.ShapeDtypeStruct((2, shards, columns, own.shape[2]), BF16),
        in_specs=[pl.BlockSpec(memory_space=pltpu.SMEM)] + [vmem] * 3,
        out_specs=vmem,
        compiler_params=VMEM,
        name="project",
    )(core, weight, own, other)


def finish_kernel(parts_ref, out_ref):
    for half in range(parts_ref.shape[0]):
        for x in range(parts_ref.shape[2]):
            total = parts_ref[half, 0, x].astype(F32)
            for y in range(1, parts_ref.shape[1]):
                total += parts_ref[half, y, x].astype(F32)
            columns = total.shape[0]
            place = (half * parts_ref.shape[2] + x) * columns
            out_ref[pl.ds(place, columns), :] = total


def turn_kernel(parts_ref, out_ref, total_ref):
    finish_kernel(parts_ref, total_ref)
    out_ref[...] = total_ref[...].T.astype(BF16)


def finish(parts):
    halves, _, x, columns, tokens = parts.shape
    total = x * halves * columns
    return pl.pallas_call(
        turn_kernel,
        out_shape=jax.ShapeDtypeStruct((tokens, total), BF16),
        scratch_shapes=[pltpu.VMEM((total, tokens), F32)],
        compiler_params=VMEM,
        name="finish",
    )(parts)


def earlier_states(state):
    rows = state.shape[0] // 8
    pieces = lax.all_to_all(state.reshape(8, rows, DH), NEAR, 0, 0)
    pieces = pieces.astype(F32)
    running = jnp.cumsum(pieces, axis=0)
    total = running[-1]
    before = running - pieces
    totals = lax.all_gather(total, "za")
    reached = jnp.arange(GRID["za"])[:, None, None] < lax.axis_index("za")
    carried = jnp.sum(jnp.where(reached, totals, 0.0), axis=0)
    prefix = (before + carried[None]).astype(BF16)
    return lax.all_to_all(prefix, NEAR, 0, 0).reshape(state.shape)


def per_device(queries, keys, values, out_weight):
    tokens, width = queries.shape
    groups = GRID["x"]
    columns = out_weight.shape[1] // groups
    weight = lax.all_to_all(out_weight.T.reshape(groups, columns, width), "x", 0, 0)
    weight = lax.all_gather(weight, ("za", "zb", "zc"))

    states = block_states(keys, values)
    index = lax.axis_index(CTX).astype(jnp.int32).reshape(1)

    def gathered(states):
        prefix = earlier_states(states)
        attended = attend(index, queries, keys, values, prefix, groups)
        return lax.all_to_all(attended, "x", 0, 0)

    def nothing(states):
        return jnp.zeros((groups, width, tokens), BF16)

    attended = lax.cond(lax.axis_index(CTX) < 64, gathered, nothing, states)
    other = lax.ppermute(attended, "core", [(0, 1), (1, 0)])
    core = lax.axis_index("core").astype(jnp.int32).reshape(1)
    partial = project(core, weight, attended, other)
    parts = lax.all_to_all(partial.reshape(32, columns, tokens), ("core",) + HEAD, 0, 0)
    return finish(parts.reshape(2, GRID["y"], GRID["x"], columns, tokens))


def solution(mesh):
    grid = Mesh(mesh.devices.reshape(tuple(GRID.values())), AXES)
    spec = P(CTX, HEAD)
    return jax.shard_map(
        per_device,
        mesh=grid,
        in_specs=(spec, spec, spec, P(HEAD, CTX)),
        out_specs=spec,
        check_vma=False,
    )
```

```python
import functools

import jax
import jax.numpy as jnp
from jax import lax
from jax.experimental import pallas as pl
from jax.experimental.pallas import tpu as pltpu
from jax.sharding import Mesh
from jax.sharding import PartitionSpec as P

DH = 128
BF16 = jnp.bfloat16
F32 = jnp.float32
GRID = {"za": 4, "zb": 2, "zc": 2, "core": 2, "y": 4, "x": 4}
AXES = tuple(GRID)
CTX = ("za", "zb", "zc", "core")
HEAD = ("y", "x")
NEAR = ("zb", "zc", "core")
VMEM = pltpu.CompilerParams(vmem_limit_bytes=32 * 1024 * 1024)


def dot(a, b, dims):
    return lax.dot_general(a, b, (dims, ((), ())), preferred_element_type=F32)


def state_kernel(k_ref, v_ref, out_ref):
    for h in range(k_ref.shape[1] // DH):
        cols = pl.ds(h * DH, DH)
        out_ref[cols, :] = dot(k_ref[:, cols], v_ref[:, cols], ((0,), (0,))).astype(BF16)


def block_states(k, v):
    return pl.pallas_call(
        state_kernel,
        out_shape=jax.ShapeDtypeStruct((k.shape[1], DH), BF16),
        compiler_params=VMEM,
        name="block_state",
    )(k, v)


def attend_kernel(index_ref, q_ref, k_ref, v_ref, prefix_ref, out_ref):
    rows = q_ref.shape[0]
    causal = lax.broadcasted_iota(jnp.int32, (rows, rows), 0) >= lax.broadcasted_iota(
        jnp.int32, (rows, rows), 1
    )
    position = index_ref[0] * rows + lax.broadcasted_iota(jnp.int32, (rows, DH), 0)
    scale = jnp.sqrt(DH * (position.astype(F32) + 1.0))
    for h in range(q_ref.shape[1] // DH):
        cols = pl.ds(h * DH, DH)
        q = q_ref[:, cols]
        scores = jnp.where(causal, dot(q, k_ref[:, cols], ((1,), (1,))), 0.0).astype(BF16)
        both = dot(scores, v_ref[:, cols], ((1,), (0,))) + dot(q, prefix_ref[cols, :], ((1,), (0,)))
        attended = (both / scale).T.astype(BF16)
        for copy in range(out_ref.shape[0]):
            out_ref[copy, cols, :] = attended


def attend(index, q, k, v, prefix, copies):
    whole = pl.BlockSpec(memory_space=pltpu.VMEM)
    return pl.pallas_call(
        attend_kernel,
        out_shape=jax.ShapeDtypeStruct((copies, q.shape[1], q.shape[0]), BF16),
        in_specs=[pl.BlockSpec(memory_space=pltpu.SMEM)] + [whole] * 4,
        out_specs=whole,
        compiler_params=VMEM,
        name="attend",
    )(index, q, k, v, prefix)


def project_kernel(core_ref, w_ref, own_ref, other_ref, out_ref):
    shards, groups, columns, width = w_ref.shape
    together = 8
    rows = together * columns
    for which, a_ref in enumerate((own_ref, other_ref)):
        place = lax.bitwise_xor(core_ref[0], which)
        for i in range(0, shards, together):
            total = dot(w_ref[i : i + together, 0].reshape(rows, width), a_ref[0], ((1,), (0,)))
            for g in range(1, groups):
                part = w_ref[i : i + together, g].reshape(rows, width)
                total += dot(part, a_ref[g], ((1,), (0,)))
            out_ref[place, i : i + together] = total.astype(BF16).reshape(together, columns, -1)


def project(core, weight, own, other):
    shards, _, columns, _ = weight.shape
    vmem = pl.BlockSpec(memory_space=pltpu.VMEM)
    return pl.pallas_call(
        project_kernel,
        out_shape=jax.ShapeDtypeStruct((2, shards, columns, own.shape[2]), BF16),
        in_specs=[pl.BlockSpec(memory_space=pltpu.SMEM)] + [vmem] * 3,
        out_specs=vmem,
        compiler_params=VMEM,
        name="project",
    )(core, weight, own, other)


def finish_kernel(parts_ref, out_ref):
    for half in range(parts_ref.shape[0]):
        for x in range(parts_ref.shape[2]):
            total = parts_ref[half, 0, x].astype(F32)
            for y in range(1, parts_ref.shape[1]):
                total += parts_ref[half, y, x].astype(F32)
            columns = total.shape[0]
            place = (half * parts_ref.shape[2] + x) * columns
            out_ref[pl.ds(place, columns), :] = total


def turn_kernel(parts_ref, out_ref, total_ref):
    finish_kernel(parts_ref, total_ref)
    out_ref[...] = total_ref[...].T.astype(BF16)


def finish(parts):
    halves, _, x, columns, tokens = parts.shape
    total = x * halves * columns
    return pl.pallas_call(
        turn_kernel,
        out_shape=jax.ShapeDtypeStruct((tokens, total), BF16),
        scratch_shapes=[pltpu.VMEM((total, tokens), F32)],
        compiler_params=VMEM,
        name="finish",
    )(parts)


def earlier_states(state):
    rows = state.shape[0] // 8
    pieces = lax.all_to_all(state.reshape(8, rows, DH), NEAR, 0, 0)
    pieces = pieces.astype(F32)
    running = jnp.cumsum(pieces, axis=0)
    total = running[-1]
    before = running - pieces
    totals = lax.all_gather(total, "za")
    reached = jnp.arange(GRID["za"])[:, None, None] < lax.axis_index("za")
    carried = jnp.sum(jnp.where(reached, totals, 0.0), axis=0)
    prefix = (before + carried[None]).astype(BF16)
    return lax.all_to_all(prefix, NEAR, 0, 0).reshape(state.shape)


def per_device(queries, keys, values, out_weight):
    tokens, width = queries.shape
    groups = GRID["x"]
    columns = out_weight.shape[1] // groups
    weight = lax.all_to_all(out_weight.T.reshape(groups, columns, width), "x", 0, 0)
    weight = lax.all_gather(weight, ("za", "zb", "zc"))

    states = block_states(keys, values)
    index = lax.axis_index(CTX).astype(jnp.int32).reshape(1)

    prefix = earlier_states(states)
    attended = attend(index, queries, keys, values, prefix, groups)
    attended = lax.all_to_all(attended, "x", 0, 0)
    other = lax.ppermute(attended, "core", [(0, 1), (1, 0)])
    core = lax.axis_index("core").astype(jnp.int32).reshape(1)
    partial = project(core, weight, attended, other)
    parts = lax.all_to_all(partial.reshape(32, columns, tokens), ("core",) + HEAD, 0, 0)
    return finish(parts.reshape(2, GRID["y"], GRID["x"], columns, tokens))


def solution(mesh):
    grid = Mesh(mesh.devices.reshape(tuple(GRID.values())), AXES)
    spec = P(CTX, HEAD)
    return jax.shard_map(
        per_device,
        mesh=grid,
        in_specs=(spec, spec, spec, P(HEAD, CTX)),
        out_specs=spec,
        check_vma=False,
    )
```

```python
import functools

import jax
import jax.numpy as jnp
from jax import lax
from jax.experimental import pallas as pl
from jax.experimental.pallas import tpu as pltpu
from jax.sharding import Mesh
from jax.sharding import PartitionSpec as P

DH = 128
BF16 = jnp.bfloat16
F32 = jnp.float32
GRID = {"za": 4, "zb": 2, "zc": 2, "core": 2, "y": 4, "xh": 2, "xl": 2}
AXES = tuple(GRID)
CTX = ("za", "zb", "zc", "core")
HEAD = ("y", "xh", "xl")
PAIRS = ("zc", "xl")
NEAR = ("zb", "zc", "core")
FAR = "za"
VMEM = pltpu.CompilerParams(vmem_limit_bytes=32 * 1024 * 1024)


def dot(a, b, dims):
    return lax.dot_general(a, b, (dims, ((), ())), preferred_element_type=F32)


def state_kernel(k_ref, v_ref, out_ref):
    for h in range(k_ref.shape[1] // DH):
        cols = pl.ds(h * DH, DH)
        out_ref[cols, :] = dot(k_ref[:, cols], v_ref[:, cols], ((0,), (0,))).astype(BF16)


def block_states(k, v):
    return pl.pallas_call(
        state_kernel,
        out_shape=jax.ShapeDtypeStruct((k.shape[1], DH), BF16),
        compiler_params=VMEM,
        name="block_state",
    )(k, v)


def attend_kernel(index_ref, q_ref, k_ref, v_ref, prefix_ref, out_ref):
    rows = q_ref.shape[0]
    causal = lax.broadcasted_iota(jnp.int32, (rows, rows), 0) >= lax.broadcasted_iota(
        jnp.int32, (rows, rows), 1
    )
    position = index_ref[0] * rows + lax.broadcasted_iota(jnp.int32, (rows, DH), 0)
    scale = jnp.sqrt(DH * (position.astype(F32) + 1.0))
    for h in range(q_ref.shape[1] // DH):
        cols = pl.ds(h * DH, DH)
        q = q_ref[:, cols]
        scores = jnp.where(causal, dot(q, k_ref[:, cols], ((1,), (1,))), 0.0).astype(BF16)
        both = dot(scores, v_ref[:, cols], ((1,), (0,))) + dot(q, prefix_ref[cols, :], ((1,), (0,)))
        attended = (both / scale).T.astype(BF16)
        for copy in range(out_ref.shape[0]):
            out_ref[copy, cols, :] = attended


def attend(index, q, k, v, prefix, copies):
    whole = pl.BlockSpec(memory_space=pltpu.VMEM)
    return pl.pallas_call(
        attend_kernel,
        out_shape=jax.ShapeDtypeStruct((copies, q.shape[1], q.shape[0]), BF16),
        in_specs=[pl.BlockSpec(memory_space=pltpu.SMEM)] + [whole] * 4,
        out_specs=whole,
        compiler_params=VMEM,
        name="attend",
    )(index, q, k, v, prefix)


def project_kernel(w_ref, a_ref, out_ref):
    pairs, halves, ends, groups, columns, width = w_ref.shape
    for t in range(a_ref.shape[0]):
        for half in range(halves):
            for end in range(ends):
                total = jnp.zeros((pairs * columns, a_ref.shape[3]), F32)
                for g in range(groups):
                    part = w_ref[:, half, end, g].reshape(pairs * columns, width)
                    total += dot(part, a_ref[t, g], ((1,), (0,)))
                out_ref[t, :, end, half] = total.astype(BF16).reshape(pairs, columns, -1)


def project(weight, attended):
    pairs, halves, ends, _, columns, _ = weight.shape
    blocks, _, _, tokens = attended.shape
    return pl.pallas_call(
        project_kernel,
        out_shape=jax.ShapeDtypeStruct((blocks, pairs, ends, halves, columns, tokens), BF16),
        compiler_params=VMEM,
        name="project",
    )(weight, attended)


def finish_kernel(parts_ref, out_ref):
    ends, ys, xhs, xls, halves, columns, _ = parts_ref.shape
    for half in range(halves):
        for end in range(ends):
            for xl in range(xls):
                total = None
                for y in range(ys):
                    for xh in range(xhs):
                        part = parts_ref[end, y, xh, xl, half].astype(F32)
                        total = part if total is None else total + part
                place = ((half * ends + end) * xls + xl) * columns
                out_ref[pl.ds(place, columns), :] = total


def turn_kernel(parts_ref, out_ref, total_ref):
    finish_kernel(parts_ref, total_ref)
    out_ref[...] = total_ref[...].T.astype(BF16)


def finish(parts):
    ends, _, _, xls, halves, columns, tokens = parts.shape
    total = ends * xls * halves * columns
    return pl.pallas_call(
        turn_kernel,
        out_shape=jax.ShapeDtypeStruct((tokens, total), BF16),
        scratch_shapes=[pltpu.VMEM((total, tokens), F32)],
        compiler_params=VMEM,
        name="finish",
    )(parts)


def earlier_states(state):
    near = lax.axis_size(NEAR)
    pieces = lax.all_to_all(state.reshape(near, state.shape[0] // near, DH), NEAR, 0, 0).astype(F32)
    running = jnp.cumsum(pieces, axis=0)
    total = running[-1]
    before = running - pieces
    totals = lax.all_gather(total.astype(BF16), FAR).astype(F32)
    reached = jnp.arange(totals.shape[0])[:, None, None] < lax.axis_index(FAR)
    carried = jnp.sum(jnp.where(reached, totals, 0.0), axis=0)
    prefix = (before + carried[None]).astype(BF16)
    return lax.all_to_all(prefix, NEAR, 0, 0).reshape(state.shape)


def per_device(queries, keys, values, out_weight):
    tokens, width = queries.shape
    groups = GRID["zc"] * GRID["xl"]
    columns = out_weight.shape[1] // groups
    weight = lax.all_to_all(out_weight.T.reshape(groups, columns, width), PAIRS, 0, 0)
    states = block_states(keys, values)
    weight, states = lax.optimization_barrier((weight, states))
    weight = lax.all_gather(weight, ("za", "zb", "core"))
    weight = weight.reshape(8, 2, GRID["zc"], GRID["xl"], columns, width)

    index = lax.axis_index(CTX).astype(jnp.int32).reshape(1)

    prefix = earlier_states(states)
    attended = attend(index, queries, keys, values, prefix, groups)
    attended = lax.all_to_all(attended, PAIRS, 0, 0)
    attended = attended.reshape(GRID["zc"], GRID["xl"], width, tokens)
    partial = project(weight, attended)
    parts = lax.all_to_all(partial.reshape(32, 2 * columns, tokens), ("zc",) + HEAD, 0, 0)
    return finish(parts.reshape(2, GRID["y"], GRID["xh"], GRID["xl"], 2, columns, tokens))


def solution(mesh):
    grid = Mesh(mesh.devices.reshape(tuple(GRID.values())), AXES)
    spec = P(CTX, HEAD)
    return jax.shard_map(
        per_device,
        mesh=grid,
        in_specs=(spec, spec, spec, P(HEAD, CTX)),
        out_specs=spec,
        check_vma=False,
    )
```

```python
import jax
import jax.numpy as jnp
from jax import lax
from jax.experimental import pallas as pl
from jax.experimental.pallas import tpu as pltpu
from jax.sharding import Mesh
from jax.sharding import PartitionSpec as P

DH = 128
BF16 = jnp.bfloat16
F32 = jnp.float32
GRID = {"za": 4, "zb": 2, "zc": 2, "core": 2, "y": 4, "xh": 2, "xl": 2}
AXES = tuple(GRID)
CTX = ("za", "zb", "zc", "core")
HEAD = ("y", "xh", "xl")
PAIRS = ("zc", "xl")
NEAR = ("zb", "zc")
FAR = "za"
VMEM = pltpu.CompilerParams(vmem_limit_bytes=32 * 1024 * 1024)


def dot(a, b, dims):
    return lax.dot_general(a, b, (dims, ((), ())), preferred_element_type=F32)


def state_kernel(k_ref, v_ref, out_ref):
    for h in range(k_ref.shape[1] // DH):
        cols = pl.ds(h * DH, DH)
        out_ref[cols, :] = dot(k_ref[:, cols], v_ref[:, cols], ((0,), (0,))).astype(BF16)


def block_states(k, v):
    return pl.pallas_call(
        state_kernel,
        out_shape=jax.ShapeDtypeStruct((k.shape[1], DH), BF16),
        compiler_params=VMEM,
        name="block_state",
    )(k, v)


def attend_kernel(index_ref, q_ref, k_ref, v_ref, prefix_ref, out_ref):
    rows = q_ref.shape[0]
    causal = lax.broadcasted_iota(jnp.int32, (rows, rows), 0) >= lax.broadcasted_iota(
        jnp.int32, (rows, rows), 1
    )
    position = index_ref[0] * rows + lax.broadcasted_iota(jnp.int32, (rows, DH), 0)
    scale = jnp.sqrt(DH * (position.astype(F32) + 1.0))
    for h in range(q_ref.shape[1] // DH):
        cols = pl.ds(h * DH, DH)
        q = q_ref[:, cols]
        scores = jnp.where(causal, dot(q, k_ref[:, cols], ((1,), (1,))), 0.0).astype(BF16)
        both = dot(scores, v_ref[:, cols], ((1,), (0,))) + dot(q, prefix_ref[cols, :], ((1,), (0,)))
        attended = (both / scale).T.astype(BF16)
        for copy in range(out_ref.shape[0]):
            out_ref[copy, cols, :] = attended


def attend(index, q, k, v, prefix, copies):
    whole = pl.BlockSpec(memory_space=pltpu.VMEM)
    return pl.pallas_call(
        attend_kernel,
        out_shape=jax.ShapeDtypeStruct((copies, q.shape[1], q.shape[0]), BF16),
        in_specs=[pl.BlockSpec(memory_space=pltpu.SMEM)] + [whole] * 4,
        out_specs=whole,
        compiler_params=VMEM,
        name="attend",
    )(index, q, k, v, prefix)


def project_kernel(w_ref, a_ref, out_ref):
    pairs, halves, ends, groups, columns, width = w_ref.shape
    for t in range(a_ref.shape[0]):
        for half in range(halves):
            for end in range(ends):
                total = jnp.zeros((pairs * columns, a_ref.shape[3]), F32)
                for g in range(groups):
                    part = w_ref[:, half, end, g].reshape(pairs * columns, width)
                    total += dot(part, a_ref[t, g], ((1,), (0,)))
                out_ref[t, :, end, half] = total.astype(BF16).reshape(pairs, columns, -1)


def project(weight, attended):
    pairs, halves, ends, _, columns, _ = weight.shape
    blocks, _, _, tokens = attended.shape
    return pl.pallas_call(
        project_kernel,
        out_shape=jax.ShapeDtypeStruct((blocks, pairs, ends, halves, columns, tokens), BF16),
        compiler_params=VMEM,
        name="project",
    )(weight, attended)


def finish_kernel(parts_ref, out_ref):
    ends, ys, xhs, xls, halves, columns, _ = parts_ref.shape
    for half in range(halves):
        for end in range(ends):
            for xl in range(xls):
                total = None
                for y in range(ys):
                    for xh in range(xhs):
                        part = parts_ref[end, y, xh, xl, half].astype(F32)
                        total = part if total is None else total + part
                place = ((half * ends + end) * xls + xl) * columns
                out_ref[pl.ds(place, columns), :] = total


def turn_kernel(parts_ref, out_ref, total_ref):
    finish_kernel(parts_ref, total_ref)
    out_ref[...] = total_ref[...].T.astype(BF16)


def finish(parts):
    ends, _, _, xls, halves, columns, tokens = parts.shape
    total = ends * xls * halves * columns
    return pl.pallas_call(
        turn_kernel,
        out_shape=jax.ShapeDtypeStruct((tokens, total), BF16),
        scratch_shapes=[pltpu.VMEM((total, tokens), F32)],
        compiler_params=VMEM,
        name="finish",
    )(parts)


def earlier_states(state):
    core = lax.axis_index("core")
    half = state.shape[0] // 2
    both = lax.all_gather(state, "core")
    mine = lax.dynamic_slice_in_dim(both, core * half, half, axis=1).astype(F32)
    chip = jnp.sum(mine, axis=0).astype(BF16)
    near = lax.axis_size(NEAR)
    pieces = lax.all_to_all(chip.reshape(near, half // near, DH), NEAR, 0, 0).astype(F32)
    running = jnp.cumsum(pieces, axis=0)
    total = running[-1]
    before = running - pieces
    totals = lax.all_gather(total.astype(BF16), FAR).astype(F32)
    reached = jnp.arange(totals.shape[0])[:, None, None] < lax.axis_index(FAR)
    carried = jnp.sum(jnp.where(reached, totals, 0.0), axis=0)
    prefix = (before + carried[None]).astype(BF16)
    prefix = lax.all_to_all(prefix, NEAR, 0, 0).reshape(half, DH)
    prefix = lax.all_gather(prefix, "core", tiled=True).astype(F32)
    return (prefix + jnp.where(core == 1, both[0].astype(F32), 0.0)).astype(BF16)


def per_device(queries, keys, values, out_weight):
    tokens, width = queries.shape
    groups = GRID["zc"] * GRID["xl"]
    columns = out_weight.shape[1] // groups
    weight = lax.all_to_all(out_weight.T.reshape(groups, columns, width), PAIRS, 0, 0)
    states = block_states(keys, values)
    weight, states = lax.optimization_barrier((weight, states))
    weight = lax.all_gather(weight, ("za", "zb", "core"))
    weight = weight.reshape(8, 2, GRID["zc"], GRID["xl"], columns, width)

    index = lax.axis_index(CTX).astype(jnp.int32).reshape(1)

    prefix = earlier_states(states)
    attended = attend(index, queries, keys, values, prefix, groups)
    attended = lax.all_to_all(attended, PAIRS, 0, 0)
    attended = attended.reshape(GRID["zc"], GRID["xl"], width, tokens)
    partial = project(weight, attended)
    parts = lax.all_to_all(partial.reshape(32, 2 * columns, tokens), ("zc",) + HEAD, 0, 0)
    return finish(parts.reshape(2, GRID["y"], GRID["xh"], GRID["xl"], 2, columns, tokens))


def solution(mesh):
    grid = Mesh(mesh.devices.reshape(tuple(GRID.values())), AXES)
    spec = P(CTX, HEAD)
    return jax.shard_map(
        per_device,
        mesh=grid,
        in_specs=(spec, spec, spec, P(HEAD, CTX)),
        out_specs=spec,
        check_vma=False,
    )
```

```python
import jax
import jax.numpy as jnp
from jax import lax
from jax.experimental import pallas as pl
from jax.experimental.pallas import tpu as pltpu
from jax.sharding import Mesh
from jax.sharding import PartitionSpec as P

DH = 128
BF16 = jnp.bfloat16
F32 = jnp.float32
GRID = {"za": 4, "zb": 2, "zc": 2, "core": 2, "y": 4, "xh": 2, "xl": 2}
AXES = tuple(GRID)
CTX = ("za", "zb", "zc", "core")
HEAD = ("y", "xh", "xl")
PAIRS = ("zc", "xl")
NEAR = ("zb", "zc", "core")
FAR = "za"
VMEM = pltpu.CompilerParams(vmem_limit_bytes=32 * 1024 * 1024)


def dot(a, b, dims):
    return lax.dot_general(a, b, (dims, ((), ())), preferred_element_type=F32)


def state_kernel(k_ref, v_ref, out_ref):
    for h in range(k_ref.shape[1] // DH):
        cols = pl.ds(h * DH, DH)
        out_ref[cols, :] = dot(k_ref[:, cols], v_ref[:, cols], ((0,), (0,))).astype(BF16)


def block_states(k, v):
    return pl.pallas_call(
        state_kernel,
        out_shape=jax.ShapeDtypeStruct((k.shape[1], DH), BF16),
        compiler_params=VMEM,
        name="block_state",
    )(k, v)


def attend_kernel(index_ref, q_ref, k_ref, v_ref, prefix_ref, out_ref):
    rows = q_ref.shape[0]
    causal = lax.broadcasted_iota(jnp.int32, (rows, rows), 0) >= lax.broadcasted_iota(
        jnp.int32, (rows, rows), 1
    )
    position = index_ref[0] * rows + lax.broadcasted_iota(jnp.int32, (rows, DH), 0)
    scale = jnp.sqrt(DH * (position.astype(F32) + 1.0))
    for h in range(q_ref.shape[1] // DH):
        cols = pl.ds(h * DH, DH)
        q = q_ref[:, cols]
        scores = jnp.where(causal, dot(q, k_ref[:, cols], ((1,), (1,))), 0.0).astype(BF16)
        both = dot(scores, v_ref[:, cols], ((1,), (0,))) + dot(q, prefix_ref[cols, :], ((1,), (0,)))
        attended = (both / scale).T.astype(BF16)
        for copy in range(out_ref.shape[0]):
            out_ref[copy, cols, :] = attended


def attend(index, q, k, v, prefix, copies):
    whole = pl.BlockSpec(memory_space=pltpu.VMEM)
    return pl.pallas_call(
        attend_kernel,
        out_shape=jax.ShapeDtypeStruct((copies, q.shape[1], q.shape[0]), BF16),
        in_specs=[pl.BlockSpec(memory_space=pltpu.SMEM)] + [whole] * 4,
        out_specs=whole,
        compiler_params=VMEM,
        name="attend",
    )(index, q, k, v, prefix)


def project_kernel(w_ref, a_ref, out_ref):
    blocks, groups, width, tokens = a_ref.shape
    _, pairs, ends, halves, columns, _ = out_ref.shape
    for t in range(blocks):
        for half in range(halves):
            for end in range(ends):
                total = jnp.zeros((pairs * columns, tokens), F32)
                for g in range(groups):
                    row = (end * groups + g) * columns
                    lanes = [(pair * halves + half) * width for pair in range(pairs)]
                    parts = [w_ref[row : row + columns, lane : lane + width] for lane in lanes]
                    total += dot(jnp.concatenate(parts, axis=0), a_ref[t, g], ((1,), (0,)))
                out_ref[t, :, end, half] = total.astype(BF16).reshape(pairs, columns, -1)


def project(weight, attended):
    blocks, groups, width, tokens = attended.shape
    columns = weight.shape[0] // (2 * groups)
    pairs = weight.shape[1] // (2 * width)
    return pl.pallas_call(
        project_kernel,
        out_shape=jax.ShapeDtypeStruct((blocks, pairs, 2, 2, columns, tokens), BF16),
        compiler_params=VMEM,
        name="project",
    )(weight, attended)


def finish_kernel(parts_ref, out_ref):
    ends, ys, xhs, xls, halves, columns, _ = parts_ref.shape
    for half in range(halves):
        for end in range(ends):
            for xl in range(xls):
                total = None
                for y in range(ys):
                    for xh in range(xhs):
                        part = parts_ref[end, y, xh, xl, half].astype(F32)
                        total = part if total is None else total + part
                place = ((half * ends + end) * xls + xl) * columns
                out_ref[pl.ds(place, columns), :] = total


def turn_kernel(parts_ref, out_ref, total_ref):
    finish_kernel(parts_ref, total_ref)
    out_ref[...] = total_ref[...].T.astype(BF16)


def finish(parts):
    ends, _, _, xls, halves, columns, tokens = parts.shape
    total = ends * xls * halves * columns
    return pl.pallas_call(
        turn_kernel,
        out_shape=jax.ShapeDtypeStruct((tokens, total), BF16),
        scratch_shapes=[pltpu.VMEM((total, tokens), F32)],
        compiler_params=VMEM,
        name="finish",
    )(parts)


def earlier_states(state):
    near = lax.axis_size(NEAR)
    pieces = lax.all_to_all(state.reshape(near, state.shape[0] // near, DH), NEAR, 0, 0).astype(F32)
    running = jnp.cumsum(pieces, axis=0)
    total = running[-1]
    before = running - pieces
    totals = lax.all_gather(total.astype(BF16), FAR).astype(F32)
    reached = jnp.arange(totals.shape[0])[:, None, None] < lax.axis_index(FAR)
    carried = jnp.sum(jnp.where(reached, totals, 0.0), axis=0)
    prefix = (before + carried[None]).astype(BF16)
    return lax.all_to_all(prefix, NEAR, 0, 0).reshape(state.shape)


def per_device(queries, keys, values, out_weight):
    tokens, width = queries.shape
    groups = GRID["zc"] * GRID["xl"]
    columns = out_weight.shape[1] // groups
    weight = lax.all_to_all(out_weight.T.reshape(groups, columns, width), PAIRS, 0, 0)
    states = block_states(keys, values)
    weight, states = lax.optimization_barrier((weight, states))
    weight = weight.reshape(groups * columns, width)
    weight = lax.all_gather(weight, ("za", "zb", "core"), axis=1, tiled=True)

    index = lax.axis_index(CTX).astype(jnp.int32).reshape(1)

    prefix = earlier_states(states)
    attended = attend(index, queries, keys, values, prefix, groups)
    attended = lax.all_to_all(attended, PAIRS, 0, 0)
    attended = attended.reshape(GRID["zc"], GRID["xl"], width, tokens)
    partial = project(weight, attended)
    parts = lax.all_to_all(partial.reshape(32, 2 * columns, tokens), ("zc",) + HEAD, 0, 0)
    return finish(parts.reshape(2, GRID["y"], GRID["xh"], GRID["xl"], 2, columns, tokens))


def solution(mesh):
    grid = Mesh(mesh.devices.reshape(tuple(GRID.values())), AXES)
    spec = P(CTX, HEAD)
    return jax.shard_map(
        per_device,
        mesh=grid,
        in_specs=(spec, spec, spec, P(HEAD, CTX)),
        out_specs=spec,
        check_vma=False,
    )
```

```python
import jax
import jax.numpy as jnp
from jax import lax
from jax.experimental import pallas as pl
from jax.experimental.pallas import tpu as pltpu
from jax.sharding import Mesh
from jax.sharding import PartitionSpec as P

DH = 128
BF16 = jnp.bfloat16
F32 = jnp.float32
GRID = {"za": 4, "zb": 2, "zc": 2, "core": 2, "y": 4, "xh": 2, "xl": 2}
AXES = tuple(GRID)
CTX = ("za", "zb", "zc", "core")
HEAD = ("y", "xh", "xl")
PAIRS = ("zc", "xl")
NEAR = ("zb", "zc", "core")
FAR = "za"
VMEM = pltpu.CompilerParams(vmem_limit_bytes=32 * 1024 * 1024)


def dot(a, b, dims):
    return lax.dot_general(a, b, (dims, ((), ())), preferred_element_type=F32)


def state_kernel(k_ref, v_ref, out_ref):
    for h in range(k_ref.shape[1] // DH):
        cols = pl.ds(h * DH, DH)
        out_ref[cols, :] = dot(k_ref[:, cols], v_ref[:, cols], ((0,), (0,))).astype(BF16)


def block_states(k, v):
    return pl.pallas_call(
        state_kernel,
        out_shape=jax.ShapeDtypeStruct((k.shape[1], DH), BF16),
        compiler_params=VMEM,
        name="block_state",
    )(k, v)


def attend_kernel(index_ref, q_ref, k_ref, v_ref, prefix_ref, out_ref):
    rows = q_ref.shape[0]
    causal = lax.broadcasted_iota(jnp.int32, (rows, rows), 0) >= lax.broadcasted_iota(
        jnp.int32, (rows, rows), 1
    )
    position = index_ref[0] * rows + lax.broadcasted_iota(jnp.int32, (rows, DH), 0)
    scale = jnp.sqrt(DH * (position.astype(F32) + 1.0))
    for h in range(q_ref.shape[1] // DH):
        cols = pl.ds(h * DH, DH)
        q = q_ref[:, cols]
        scores = jnp.where(causal, dot(q, k_ref[:, cols], ((1,), (1,))), 0.0).astype(BF16)
        both = dot(scores, v_ref[:, cols], ((1,), (0,))) + dot(q, prefix_ref[cols, :], ((1,), (0,)))
        attended = (both / scale).T.astype(BF16)
        for copy in range(out_ref.shape[0]):
            out_ref[copy, cols, :] = attended


def attend(index, q, k, v, prefix, copies):
    whole = pl.BlockSpec(memory_space=pltpu.VMEM)
    return pl.pallas_call(
        attend_kernel,
        out_shape=jax.ShapeDtypeStruct((copies, q.shape[1], q.shape[0]), BF16),
        in_specs=[pl.BlockSpec(memory_space=pltpu.SMEM)] + [whole] * 4,
        out_specs=whole,
        compiler_params=VMEM,
        name="attend",
    )(index, q, k, v, prefix)


def project_kernel(w_ref, a_ref, out_ref):
    blocks, groups, width, tokens = a_ref.shape
    _, pairs, ends, halves, columns, _ = out_ref.shape
    for t in range(blocks):
        for half in range(halves):
            for end in range(ends):
                total = jnp.zeros((pairs * columns, tokens), F32)
                for g in range(groups):
                    row = (end * groups + g) * columns
                    lanes = [(half * pairs + pair) * width for pair in range(pairs)]
                    parts = [w_ref[row : row + columns, lane : lane + width] for lane in lanes]
                    total += dot(jnp.concatenate(parts, axis=0), a_ref[t, g], ((1,), (0,)))
                out_ref[t, :, end, half] = total.astype(BF16).reshape(pairs, columns, -1)


def project(weight, attended):
    blocks, groups, width, tokens = attended.shape
    columns = weight.shape[0] // (2 * groups)
    pairs = weight.shape[1] // (2 * width)
    return pl.pallas_call(
        project_kernel,
        out_shape=jax.ShapeDtypeStruct((blocks, pairs, 2, 2, columns, tokens), BF16),
        compiler_params=VMEM,
        name="project",
    )(weight, attended)


def finish_kernel(parts_ref, out_ref):
    ends, ys, xhs, xls, halves, columns, _ = parts_ref.shape
    for half in range(halves):
        for end in range(ends):
            for xl in range(xls):
                total = None
                for y in range(ys):
                    for xh in range(xhs):
                        part = parts_ref[end, y, xh, xl, half].astype(F32)
                        total = part if total is None else total + part
                place = ((half * ends + end) * xls + xl) * columns
                out_ref[pl.ds(place, columns), :] = total


def turn_kernel(parts_ref, out_ref, total_ref):
    finish_kernel(parts_ref, total_ref)
    out_ref[...] = total_ref[...].T.astype(BF16)


def finish(parts):
    ends, _, _, xls, halves, columns, tokens = parts.shape
    total = ends * xls * halves * columns
    return pl.pallas_call(
        turn_kernel,
        out_shape=jax.ShapeDtypeStruct((tokens, total), BF16),
        scratch_shapes=[pltpu.VMEM((total, tokens), F32)],
        compiler_params=VMEM,
        name="finish",
    )(parts)


def earlier_states(state):
    near = lax.axis_size(NEAR)
    pieces = lax.all_to_all(state.reshape(near, state.shape[0] // near, DH), NEAR, 0, 0).astype(F32)
    running = jnp.cumsum(pieces, axis=0)
    total = running[-1]
    before = running - pieces
    totals = lax.all_gather(total.astype(BF16), FAR).astype(F32)
    reached = jnp.arange(totals.shape[0])[:, None, None] < lax.axis_index(FAR)
    carried = jnp.sum(jnp.where(reached, totals, 0.0), axis=0)
    prefix = (before + carried[None]).astype(BF16)
    return lax.all_to_all(prefix, NEAR, 0, 0).reshape(state.shape)


def per_device(queries, keys, values, out_weight):
    tokens, width = queries.shape
    groups = GRID["zc"] * GRID["xl"]
    columns = out_weight.shape[1] // groups
    weight = lax.all_to_all(out_weight.T.reshape(groups, columns, width), PAIRS, 0, 0)
    states = block_states(keys, values)
    weight, states = lax.optimization_barrier((weight, states))
    weight = weight.reshape(groups * columns, width)
    weight = lax.all_gather(weight, ("core", "za", "zb"), axis=1, tiled=True)

    index = lax.axis_index(CTX).astype(jnp.int32).reshape(1)

    prefix = earlier_states(states)
    attended = attend(index, queries, keys, values, prefix, groups)
    attended = lax.all_to_all(attended, PAIRS, 0, 0)
    attended = attended.reshape(GRID["zc"], GRID["xl"], width, tokens)
    partial = project(weight, attended)
    parts = lax.all_to_all(partial.reshape(32, 2 * columns, tokens), ("zc",) + HEAD, 0, 0)
    return finish(parts.reshape(2, GRID["y"], GRID["xh"], GRID["xl"], 2, columns, tokens))


def solution(mesh):
    grid = Mesh(mesh.devices.reshape(tuple(GRID.values())), AXES)
    spec = P(CTX, HEAD)
    return jax.shard_map(
        per_device,
        mesh=grid,
        in_specs=(spec, spec, spec, P(HEAD, CTX)),
        out_specs=spec,
        check_vma=False,
    )
```
